512 devices in a mesh: tm: 512 (over y, x, z, core).
Axes of the slice: x: 4, y: 8, z: 8, core: 2. Of those that a mesh axis runs over, the one named last changes fastest.
Arguments:
- inputs: float32 [256, 131072], P(None, 'tm'), may hold values from -6 to 6
- cotangent: float32 [256, 131072], P(None, 'tm'), may hold values from -6 to 6
- taps_far: float32 [3, 256, 256], replicated, may hold values from -0.21875 to 0.21875
- taps_near: float32 [3, 256, 256], replicated, may hold values from -0.21875 to 0.21875
- joining: float32 [256, 512], replicated, may hold values from -0.25 to 0.25
Outputs:
- input_grad: float32 [256, 131072], P(None, 'tm')
- far_grad: float32 [3, 256, 256], replicated
- near_grad: float32 [3, 256, 256], replicated
- joining_grad: float32 [256, 512], replicated
The draws below stay inside these ranges and needn't reach their ends.
All inputs are finite; a program needn't handle non-finite values.
Results may differ from the reference program's by a relative error of at most 0.000071.
Values sent between devices are 32-bit elements; how exact they have to be, the bound alone decides.
A program may use at most 64 MiB of HBM per device.

```python
import jax
import jax.numpy as jnp
from jax import lax

C = 256
NEAR = 4
TIME = 131072
FAR = 16384


def block_levels(stream_key, shape, pieces, low, largest):
    level = 1.0
    for dim, parts in pieces:
        draws = jax.random.uniform(jax.random.fold_in(jax.random.fold_in(stream_key, 6), dim), (parts,), jnp.float32, low / len(pieces), largest / len(pieces))
        level = level * jnp.repeat(jnp.exp(draws), shape[dim] // parts).reshape((-1,) + (1,) * (len(shape) - 1 - dim))
    return level


def noise(own_key, dims, width, reach, split=(), held_as=jnp.bfloat16):
    loudness = block_levels(own_key, dims, split, -0.22, 0.18) if split else 1.0
    drawn = jax.random.normal(own_key, dims, jnp.float32) * width * loudness
    return jnp.minimum(jnp.maximum(drawn, -reach), reach).astype(held_as)


def setup_inputs(seed: int = 0) -> dict:
    key_of = jax.random.split(jax.random.key(seed), 6)
    inputs = noise(key_of[0], (C, TIME), 1.0, 6.0, ((1, 512),), jnp.float32)
    cotangent = noise(key_of[1], (C, TIME), 1.0, 6.0, ((1, 512),), jnp.float32)
    taps_far = noise(key_of[2], (3, C, C), (3 * C) ** -0.5, 0.21875, (), jnp.float32)
    taps_near = noise(key_of[3], (3, C, C), (3 * C) ** -0.5, 0.21875, (), jnp.float32)
    joining = noise(key_of[4], (C, 2 * C), (2 * C) ** -0.5, 0.25, (), jnp.float32)
    return dict(inputs=inputs, cotangent=cotangent, taps_far=taps_far, taps_near=taps_near, joining=joining)


def product(left, right):
    return jnp.dot(left, right, precision=lax.Precision.HIGHEST, preferred_element_type=jnp.float32)

def before(field, shift_by):
    return jnp.pad(field[:, :-shift_by], ((0, 0), (shift_by, 0)))

def after(field, shift_by):
    return jnp.pad(field[:, shift_by:], ((0, 0), (0, shift_by)))

def gelu_slope(value):
    inner = 0.7978845608 * (value + 0.044715 * value * value * value)
    hyper = jnp.tanh(inner)
    return 0.5 * (1.0 + hyper) + 0.5 * value * (1.0 - hyper * hyper) * 0.7978845608 * (1.0 + 3.0 * 0.044715 * value * value)

def reference(inputs, cotangent, taps_far, taps_near, joining):
    far_prev = before(inputs, FAR)
    far_next = after(inputs, FAR)
    near_prev = before(inputs, NEAR)
    near_next = after(inputs, NEAR)
    branch_far = product(taps_far[0], far_prev) + product(taps_far[1], inputs) + product(taps_far[2], far_next)
    branch_near = product(taps_near[0], near_prev) + product(taps_near[1], inputs) + product(taps_near[2], near_next)
    zvalue = product(joining[:, :C], branch_far) + product(joining[:, C:], branch_near)
    dzvalue = cotangent * gelu_slope(zvalue)
    d_far = product(joining[:, :C].T, dzvalue)
    d_near = product(joining[:, C:].T, dzvalue)
    input_grad = cotangent + product(taps_far[0].T, after(d_far, FAR)) + product(taps_far[1].T, d_far) + product(taps_far[2].T, before(d_far, FAR))
    input_grad = input_grad + product(taps_near[0].T, after(d_near, NEAR)) + product(taps_near[1].T, d_near) + product(taps_near[2].T, before(d_near, NEAR))
    scale = 1.0 / jnp.sqrt(jnp.float32(TIME))
    far_grad = jnp.stack([product(d_far, far_prev.T), product(d_far, inputs.T), product(d_far, far_next.T)]) * scale
    near_grad = jnp.stack([product(d_near, near_prev.T), product(d_near, inputs.T), product(d_near, near_next.T)]) * scale
    joining_grad = jnp.concatenate([product(dzvalue, branch_far.T), product(dzvalue, branch_near.T)], axis=1) * scale
    return (input_grad, far_grad, near_grad, joining_grad)
```

```python
import functools
import math

import jax
import jax.numpy as jnp
from jax import lax
from jax.experimental import pallas as pl
from jax.experimental.pallas import tpu as pltpu
from jax.sharding import PartitionSpec as P

NEAR = 4
C = 256
L = 128
Y, X, Z = 8, 4, 8
MESH = pl.DeviceIdType.MESH
F32 = jnp.float32
BF16 = jnp.bfloat16
NA = 96 // (X * Z)
NB = 64 // (X * Z)
GA, GB = NA * Z, NB * X
NN = (((1,), (0,)), ((), ()))
NT = (((1,), (1,)), ((), ()))


def split(v):
    hi = v.astype(BF16)
    return hi, (v - hi.astype(F32)).astype(BF16)


def mm3(a, b, dims):
    dot = functools.partial(lax.dot_general, dimension_numbers=dims, preferred_element_type=F32)
    return dot(a[0], b[0]) + (dot(a[0], b[1]) + dot(a[1], b[0]))


def gelu_slope(value):
    inner = 0.7978845608 * (value + 0.044715 * value * value * value)
    hyper = jnp.tanh(inner)
    return 0.5 * (1.0 + hyper) + 0.5 * value * (1.0 - hyper * hyper) * 0.7978845608 * (
        1.0 + 3.0 * 0.044715 * value * value
    )


def shifted(b0, b1, p, n):
    lane = lax.broadcasted_iota(jnp.int32, (C, L), 1)
    low, high = lane < NEAR, lane >= L - NEAR
    r0, r1, rp = (pltpu.roll(v, NEAR, 1) for v in (b0, b1, p))
    s0, s1, sn = (pltpu.roll(v, L - NEAR, 1) for v in (b0, b1, n))
    back = jnp.concatenate([jnp.where(low, rp, r0), jnp.where(low, r0, r1)], axis=1)
    ahead = jnp.concatenate([jnp.where(high, s1, s0), jnp.where(high, sn, s1)], axis=1)
    return back, ahead


def kernel(
    scale,
    x_in, cot_in, tf_in, tn_in, j_in,
    ig_out, far_out, near_out, join_out,
    xv, cotv, tfv, tnv, jv,
    xfar, xnear, dfar, dnear, dz,
    xh, xl, ah, al, th, tl, ath, atl, jth, jtl, dh, dl, zacc, igv,
    s0, s1, rc, ra1, rb1, s2a, s2b, ra2, rb2, ry, full,
    farv, nearv, joinv,
    lsem, osem, xs, xr, ds, dr, cs, cr,
    as1, ar1, bs1, br1, as2, ar2, bs2, br2, ys, yr,
    gas1, gar1, gbs1, gbr1, gas2, gar2, gbs2, gbr2, fas, far_, fbs, fbr,
):
    me = lax.axis_index("tm")
    c = lax.rem(me, 2)
    z = lax.rem(me // 2, Z)
    x = lax.rem(me // (2 * Z), X)
    y = me // (2 * Z * X)
    total = 2 * X * Y * Z

    def at(yy, xx, zz, cc):
        return ((yy * X + xx) * Z + zz) * 2 + cc

    def ypeer(d):
        return at(lax.rem(y + d, Y), x, z, c)

    def xpeer(d):
        return at(y, lax.rem(x + d, X), z, c)

    def zpeer(d):
        return at(y, x, lax.rem(z + d, Z), c)

    sibling = at(y, x, z, 1 - c)
    later, earlier = lax.rem(me + 1, total), lax.rem(me + total - 1, total)
    ys_, xs_, zs_ = range(1, Y), range(1, X), range(1, Z)
    zorder = [4, 3, 5, 2, 6, 1, 7]
    yorder = [4, 3, 5, 2, 6, 1, 7]
    xorder = [2, 1, 3]
    started = []

    def send(src, dst, ssem, rsem, device):
        copy = pltpu.make_async_remote_copy(
            src_ref=src, dst_ref=dst, send_sem=ssem, recv_sem=rsem, device_id=(device,), device_id_type=MESH
        )
        copy.start()
        started.append(copy)
        return copy

    def local(src, dst, sem):
        copy = pltpu.make_async_copy(src, dst, sem)
        copy.start()
        return copy

    partners = [ypeer(d) for d in ys_] + [xpeer(d) for d in xs_] + [zpeer(d) for d in zs_] + [later, earlier]
    barrier = pltpu.get_barrier_semaphore()
    for partner in partners + [at(y, x, z, 1 - c)]:
        pl.semaphore_signal(barrier, inc=1, device_id=(partner,), device_id_type=MESH)
    loads = [
        local(src, dst, lsem.at[k])
        for k, (src, dst) in enumerate(
            [(j_in, jv), (tf_in, tfv), (tn_in, tnv), (x_in, xv), (cot_in, cotv)]
        )
    ]
    pl.semaphore_wait(barrier, len(partners) + 1)

    up, down = ypeer(1), ypeer(Y - 1)
    xf = [
        send(x_in, xfar.at[0], xs.at[0], xr.at[0], up),
        send(x_in, xfar.at[1], xs.at[1], xr.at[1], down),
    ]
    xn = [
        send(x_in.at[:, pl.ds(L, L)], xnear.at[0], xs.at[2], xr.at[2], later),
        send(x_in.at[:, pl.ds(0, L)], xnear.at[1], xs.at[3], xr.at[3], earlier),
    ]
    one = lambda ok: jnp.where(ok, 1.0, 0.0).astype(F32)
    has_up, has_down = one(y < Y - 1), one(y > 0)
    has_later, has_earlier = one(me < total - 1), one(me > 0)

    def put(hi, lo, k, v):
        hi[k], lo[k] = split(v)

    def get(hi, lo, k):
        return hi[k], lo[k]

    for copy in loads[:3]:
        copy.wait()
    jf, jn = split(jv[:, :C]), split(jv[:, C:])
    for k in range(3):
        put(th, tl, k, tfv[k])
        put(th, tl, 3 + k, tnv[k])
    joined = [
        mm3(jf, get(th, tl, 0), NN),
        mm3(jf, get(th, tl, 1), NN) + mm3(jn, get(th, tl, 4), NN),
        mm3(jf, get(th, tl, 2), NN),
        mm3(jn, get(th, tl, 3), NN),
        mm3(jn, get(th, tl, 5), NN),
    ]
    for k, v in enumerate(joined):
        put(ah, al, k, v)
    for copy in loads[3:]:
        copy.wait()
    put(xh, xl, 1, xv[...])
    xn[0].wait_recv()
    xn[1].wait_recv()
    back, ahead = shifted(xv[:, :L], xv[:, L:], xnear[0] * has_earlier, xnear[1] * has_later)
    put(xh, xl, 3, back)
    put(xh, xl, 4, ahead)
    zacc[...] = sum(mm3(get(ah, al, k), get(xh, xl, k), NN) for k in (1, 3, 4))
    for k, v in enumerate(joined):
        put(ath, atl, k, v.T)
    put(jth, jtl, 0, jv[:, :C].T)
    put(jth, jtl, 1, jv[:, C:].T)

    xf[0].wait_recv()
    put(xh, xl, 0, xfar[0] * has_down)
    xf[1].wait_recv()
    put(xh, xl, 2, xfar[1] * has_up)
    zvalue = zacc[...] + (mm3(get(ah, al, 0), get(xh, xl, 0), NN) + mm3(get(ah, al, 2), get(xh, xl, 2), NN))
    dzvalue = cotv[...] * gelu_slope(zvalue)
    dz[...] = dzvalue
    dh[...], dl[...] = split(dzvalue)
    df = [
        send(dz, dfar.at[0], ds.at[0], dr.at[0], up),
        send(dz, dfar.at[1], ds.at[1], dr.at[1], down),
    ]

    for half, out in ((1 - c, s1), (c, s0)):
        rows = pl.ds(pl.multiple_of(half * L, L), L)
        part = dh[rows, :], dl[rows, :]
        for k in range(5):
            g = mm3(part, get(xh, xl, k), NT)
            out[pl.ds(32 * k, 16)] = g[:, :L].reshape(16, 8, L)
            out[pl.ds(32 * k + 16, 16)] = g[:, L:].reshape(16, 8, L)
        if out is s1:
            core = [send(s1, rc, cs.at[0], cr.at[0], sibling)]
    dn = [
        send(dz.at[:, pl.ds(L, L)], dnear.at[0], ds.at[2], dr.at[2], later),
        send(dz.at[:, pl.ds(0, L)], dnear.at[1], ds.at[3], dr.at[3], earlier),
    ]
    core[0].wait_recv()
    s0[...] = s0[...] + rc[...]

    p1a = [
        send(s0.at[pl.ds(GA * lax.rem(x + d, X), GA)], ra1.at[d - 1], as1.at[d - 1], ar1.at[d - 1], xpeer(d))
        for d in xorder
    ]
    p1b = [
        send(s0.at[pl.ds(96 + GB * lax.rem(z + d, Z), GB)], rb1.at[d - 1], bs1.at[d - 1], br1.at[d - 1], zpeer(d))
        for d in zorder
    ]
    igv[...] = cotv[...] + mm3(get(ath, atl, 1), (dh[...], dl[...]), NN)
    for copy in p1a:
        copy.wait_recv()
    s2a[...] = s0[pl.ds(GA * x, GA)] + sum(ra1[d - 1] for d in xs_)
    p2a = [
        send(s2a.at[pl.ds(NA * lax.rem(z + d, Z), NA)], ra2.at[d - 1], as2.at[d - 1], ar2.at[d - 1], zpeer(d))
        for d in zorder
    ]
    for copy in p1b:
        copy.wait_recv()
    s2b[...] = s0[pl.ds(96 + GB * z, GB)] + sum(rb1[d - 1] for d in zs_)
    p2b = [
        send(s2b.at[pl.ds(NB * lax.rem(x + d, X), NB)], rb2.at[d - 1], bs2.at[d - 1], br2.at[d - 1], xpeer(d))
        for d in xorder
    ]

    dn[0].wait_recv()
    dn[1].wait_recv()
    back, ahead = shifted(dz[:, :L], dz[:, L:], dnear[0] * has_earlier, dnear[1] * has_later)
    acc = mm3(get(ath, atl, 3), split(ahead), NN) + mm3(get(ath, atl, 4), split(back), NN)
    df[0].wait_recv()
    df[1].wait_recv()
    acc += mm3(get(ath, atl, 0), split(dfar[1] * has_up), NN) + mm3(get(ath, atl, 2), split(dfar[0] * has_down), NN)
    igv[...] = igv[...] + acc
    outs = [local(igv, ig_out, osem.at[0])]

    for copy in p2a + p2b:
        copy.wait_recv()
    mine = ry.at[y]
    mine[pl.ds(0, NA)] = s2a[pl.ds(NA * z, NA)] + sum(ra2[d - 1] for d in zs_)
    mine[pl.ds(NA, NB)] = s2b[pl.ds(NB * x, NB)] + sum(rb2[d - 1] for d in xs_)
    p3 = [send(mine, ry.at[y], ys.at[d - 1], yr.at[d - 1], ypeer(d)) for d in yorder]
    for copy in p3:
        copy.wait_recv()
    summed = ry[0]
    for k in range(1, Y):
        summed = summed + ry[k]
    fa = full.at[c, pl.ds(GA * x + NA * z, NA)]
    fb = full.at[c, pl.ds(96 + GB * z + NB * x, NB)]
    fa[...] = summed[:NA]
    fb[...] = summed[NA:]

    g1a = [send(fa, fa, gas1.at[d - 1], gar1.at[d - 1], zpeer(d)) for d in zorder]
    g1b = [send(fb, fb, gbs1.at[d - 1], gbr1.at[d - 1], xpeer(d)) for d in xorder]

    def block_a(xx):
        return full.at[c, pl.ds(GA * xx, GA)]

    def block_b(zz):
        return full.at[c, pl.ds(96 + GB * zz, GB)]

    for copy in g1a:
        copy.wait_recv()
    g2a = {d: send(block_a(x), block_a(x), gas2.at[d - 1], gar2.at[d - 1], xpeer(d)) for d in xorder}
    for copy in g1b:
        copy.wait_recv()
    g2b = {d: send(block_b(z), block_b(z), gbs2.at[d - 1], gbr2.at[d - 1], zpeer(d)) for d in zorder}
    forward_a = [send(block_a(x), block_a(x), fas.at[0], far_.at[0], sibling)]
    forward_b = [send(block_b(z), block_b(z), fbs.at[0], fbr.at[0], sibling)]
    for d in (1, 3, 2):
        g2a[d].wait_recv()
        block = block_a(lax.rem(x - d + X, X))
        forward_a.append(send(block, block, fas.at[d], far_.at[d], sibling))
    for d in (1, 7, 2, 6, 3, 5, 4):
        g2b[d].wait_recv()
        block = block_b(lax.rem(z - d + Z, Z))
        forward_b.append(send(block, block, fbs.at[d], fbr.at[d], sibling))
    for copy in forward_a:
        copy.wait_recv()

    def gathered(k):
        rows = [
            jnp.concatenate([full[h, pl.ds(32 * k + 16 * q, 16)].reshape(L, L) for q in (0, 1)], axis=1)
            for h in (0, 1)
        ]
        return split(jnp.concatenate(rows, axis=0))

    def grads(js, terms, out, jout, col):
        jacc = None
        for k, tap, slot in terms:
            g = gathered(k)
            out[slot] = mm3(get(jth, jtl, js), g, NN) * scale
            term = mm3(g, get(th, tl, tap), NT)
            jacc = term if jacc is None else jacc + term
        jout[:, col : col + C] = jacc * scale

    grads(0, [(0, 0, 0), (1, 1, 1), (2, 2, 2)], farv, joinv, 0)
    outs.append(local(farv, far_out, osem.at[1]))
    for copy in forward_b:
        copy.wait_recv()
    grads(1, [(3, 3, 0), (1, 4, 1), (4, 5, 2)], nearv, joinv, C)
    outs.append(local(nearv, near_out, osem.at[2]))
    outs.append(local(joinv, join_out, osem.at[3]))
    for copy in started:
        copy.wait_send()
    for copy in outs:
        copy.wait()


def on_device(inputs, cotangent, taps_far, taps_near, joining):
    scale = 1.0 / math.sqrt(inputs.shape[1] * lax.axis_size("tm"))
    sq = (C, C)
    vm = lambda *shape: pltpu.VMEM(shape, F32)
    vb = lambda *shape: pltpu.VMEM(shape, BF16)
    dma = lambda n: pltpu.SemaphoreType.DMA((n,))
    anywhere = pl.BlockSpec(memory_space=pl.ANY)
    scratch = (
        [vm(*sq), vm(*sq), vm(3, *sq), vm(3, *sq), vm(C, 2 * C)]
        + [vm(2, *sq), vm(2, C, L), vm(2, *sq), vm(2, C, L), vm(*sq)]
        + [vb(5, *sq)] * 4 + [vb(6, *sq)] * 2 + [vb(5, *sq)] * 2 + [vb(2, *sq)] * 2 + [vb(*sq)] * 2
        + [vm(*sq), vm(*sq)]
        + [vm(160, 8, L)] * 3
        + [vm(X - 1, GA, 8, L), vm(Z - 1, GB, 8, L), vm(GA, 8, L), vm(GB, 8, L)]
        + [vm(Z - 1, NA, 8, L), vm(X - 1, NB, 8, L), vm(Y, NA + NB, 8, L), vm(2, 160, 8, L)]
        + [vm(3, *sq), vm(3, *sq), vm(C, 2 * C)]
        + [dma(5), dma(4), dma(4), dma(4), dma(4), dma(4), dma(1), dma(1)]
        + [dma(X - 1)] * 2 + [dma(Z - 1)] * 2 + [dma(Z - 1)] * 2 + [dma(X - 1)] * 2 + [dma(Y - 1)] * 2
        + [dma(Z - 1)] * 2 + [dma(X - 1)] * 2 + [dma(X - 1)] * 2 + [dma(Z - 1)] * 2
        + [dma(X)] * 2 + [dma(Z)] * 2
    )
    return pl.pallas_call(
        functools.partial(kernel, scale),
        out_shape=[
            jax.ShapeDtypeStruct(sq, F32),
            jax.ShapeDtypeStruct((3, *sq), F32),
            jax.ShapeDtypeStruct((3, *sq), F32),
            jax.ShapeDtypeStruct((C, 2 * C), F32),
        ],
        in_specs=[anywhere] * 5,
        out_specs=[anywhere] * 4,
        scratch_shapes=scratch,
        compiler_params=pltpu.CompilerParams(
            collective_id=0, has_side_effects=True, vmem_limit_bytes=48 * 1024 * 1024
        ),
    )(inputs, cotangent, taps_far, taps_near, joining)


def solution(mesh):
    in_specs = (P(None, "tm"), P(None, "tm"), P(), P(), P())
    out_specs = (P(None, "tm"), P(), P(), P())
    return jax.shard_map(
        on_device, mesh=mesh, in_specs=in_specs, out_specs=out_specs, check_vma=False
    )
```

```python
import functools
import math

import jax
import jax.numpy as jnp
from jax import lax
from jax.experimental import pallas as pl
from jax.experimental.pallas import tpu as pltpu
from jax.sharding import PartitionSpec as P

NEAR = 4
C = 256
L = 128
Y, X, Z = 8, 4, 8
MESH = pl.DeviceIdType.MESH
F32 = jnp.float32
BF16 = jnp.bfloat16
M = 32
NA = 4 * M // (X * Z)
NB = M // (X * Z)
B0 = 4 * M
GA, GB = NA * Z, NB * X
NN = (((1,), (0,)), ((), ()))
NT = (((1,), (1,)), ((), ()))


def split(v):
    hi = v.astype(BF16)
    return hi, (v - hi.astype(F32)).astype(BF16)


def mm3(a, b, dims):
    dot = functools.partial(lax.dot_general, dimension_numbers=dims, preferred_element_type=F32)
    both = dot(jnp.concatenate(a, axis=0), b[0])
    return both[:C] + (both[C:] + dot(a[0], b[1]))


def gelu_slope(value):
    inner = 0.7978845608 * (value + 0.044715 * value * value * value)
    hyper = jnp.tanh(inner)
    return 0.5 * (1.0 + hyper) + 0.5 * value * (1.0 - hyper * hyper) * 0.7978845608 * (
        1.0 + 3.0 * 0.044715 * value * value
    )


def shifted(b0, b1, p, n):
    lane = lax.broadcasted_iota(jnp.int32, (C, L), 1)
    low, high = lane < NEAR, lane >= L - NEAR
    r0, r1, rp = (pltpu.roll(v, NEAR, 1) for v in (b0, b1, p))
    s0, s1, sn = (pltpu.roll(v, L - NEAR, 1) for v in (b0, b1, n))
    back = jnp.concatenate([jnp.where(low, rp, r0), jnp.where(low, r0, r1)], axis=1)
    ahead = jnp.concatenate([jnp.where(high, s1, s0), jnp.where(high, sn, s1)], axis=1)
    return back, ahead


def gathered(full, scale, k):
    rows = [
        jnp.concatenate([full[h, pl.ds(M * k + 16 * q, 16)].reshape(L, L) for q in (0, 1)], axis=1)
        for h in (0, 1)
    ]
    return split(jnp.concatenate(rows, axis=0) * scale)


def kernel(
    scale,
    x_in, cot_in, tf_in, tn_in, j_in,
    igv, grads, joins, full, th, tl, jth, jtl,
    xv, cotv, tfv, tnv, jv,
    xfar, xnear, dfar, dnear, dz,
    xh, xl, ah, al, ath, atl, dhl, zacc,
    sums, rc, ra1, rb1, s2a, s2b, ra2, rb2, ry,
    lsem, xs, xr, ds, dr, cs, cr,
    as1, ar1, bs1, br1, as2, ar2, bs2, br2, ys, yr,
    gas1, gar1, gbs1, gbr1, gas2, gar2, gbs2, gbr2, fas, far_, fbs, fbr,
):
    me = lax.axis_index("tm")
    c = lax.rem(me, 2)
    z = lax.rem(me // 2, Z)
    x = lax.rem(me // (2 * Z), X)
    y = me // (2 * Z * X)
    total = 2 * X * Y * Z

    def at(yy, xx, zz, cc):
        return ((yy * X + xx) * Z + zz) * 2 + cc

    def ypeer(d):
        return at(lax.rem(y + d, Y), x, z, c)

    def xpeer(d):
        return at(y, lax.rem(x + d, X), z, c)

    def zpeer(d):
        return at(y, x, lax.rem(z + d, Z), c)

    sibling = at(y, x, z, 1 - c)
    later, earlier = lax.rem(me + 1, total), lax.rem(me + total - 1, total)
    ys_, xs_, zs_ = range(1, Y), range(1, X), range(1, Z)
    zorder = [4, 3, 5, 2, 6, 1, 7]
    yorder = [4, 3, 5, 2, 6, 1, 7]
    xorder = [2, 1, 3]
    started = []

    def send(src, dst, ssem, rsem, device):
        copy = pltpu.make_async_remote_copy(
            src_ref=src, dst_ref=dst, send_sem=ssem, recv_sem=rsem, device_id=(device,), device_id_type=MESH
        )
        copy.start()
        started.append(copy)
        return copy

    def local(src, dst, sem):
        copy = pltpu.make_async_copy(src, dst, sem)
        copy.start()
        return copy

    partners = [ypeer(d) for d in ys_] + [xpeer(d) for d in xs_] + [zpeer(d) for d in zs_] + [later, earlier]
    barrier = pltpu.get_barrier_semaphore()
    for partner in partners + [at(y, x, z, 1 - c)]:
        pl.semaphore_signal(barrier, inc=1, device_id=(partner,), device_id_type=MESH)
    loads = [
        local(src, dst, lsem.at[k])
        for k, (src, dst) in enumerate(
            [(j_in, jv), (tf_in, tfv), (tn_in, tnv), (x_in, xv), (cot_in, cotv)]
        )
    ]
    pl.semaphore_wait(barrier, len(partners) + 1)

    up, down = ypeer(1), ypeer(Y - 1)
    xf = [
        send(x_in, xfar.at[0], xs.at[0], xr.at[0], up),
        send(x_in, xfar.at[1], xs.at[1], xr.at[1], down),
    ]
    xn = [
        send(x_in.at[:, pl.ds(L, L)], xnear.at[0], xs.at[2], xr.at[2], later),
        send(x_in.at[:, pl.ds(0, L)], xnear.at[1], xs.at[3], xr.at[3], earlier),
    ]
    one = lambda ok: jnp.where(ok, 1.0, 0.0).astype(F32)
    has_up, has_down = one(y < Y - 1), one(y > 0)
    has_later, has_earlier = one(me < total - 1), one(me > 0)

    def put(hi, lo, k, v):
        hi[k], lo[k] = split(v)

    def get(hi, lo, k):
        return hi[k], lo[k]

    for copy in loads[:3]:
        copy.wait()
    jf, jn = split(jv[:, :C]), split(jv[:, C:])
    for k in range(3):
        put(th, tl, k, tfv[k])
        put(th, tl, 3 + k, tnv[k])
    joined = [
        mm3(jf, get(th, tl, 0), NN),
        mm3(jf, get(th, tl, 2), NN),
        mm3(jn, get(th, tl, 3), NN),
        mm3(jn, get(th, tl, 5), NN),
        mm3(jf, get(th, tl, 1), NN) + mm3(jn, get(th, tl, 4), NN),
    ]
    for k, v in enumerate(joined):
        put(ah, al, k, v)
    for copy in loads[3:]:
        copy.wait()
    put(xh, xl, 4, xv[...])
    xn[0].wait_recv()
    xn[1].wait_recv()
    back, ahead = shifted(xv[:, :L], xv[:, L:], xnear[0] * has_earlier, xnear[1] * has_later)
    put(xh, xl, 2, back)
    put(xh, xl, 3, ahead)
    zacc[...] = sum(mm3(get(ah, al, k), get(xh, xl, k), NN) for k in (4, 2, 3))
    for k, v in enumerate(joined):
        put(ath, atl, k, v.T)
    put(jth, jtl, 0, jv[:, :C].T)
    put(jth, jtl, 1, jv[:, C:].T)

    xf[0].wait_recv()
    put(xh, xl, 0, xfar[0] * has_down)
    xf[1].wait_recv()
    put(xh, xl, 1, xfar[1] * has_up)
    zvalue = zacc[...] + (mm3(get(ah, al, 0), get(xh, xl, 0), NN) + mm3(get(ah, al, 1), get(xh, xl, 1), NN))
    dzvalue = cotv[...] * gelu_slope(zvalue)
    dz[...] = dzvalue
    dhl[pl.ds(0, C)], dhl[pl.ds(C, C)] = split(dzvalue)
    df = [
        send(dz, dfar.at[0], ds.at[0], dr.at[0], up),
        send(dz, dfar.at[1], ds.at[1], dr.at[1], down),
    ]

    order = [4] + [lax.rem(x + d, X) for d in xorder] + [x]
    core, p1a, p1b = [], [], []

    def multiply(i, k):
        hilo = lax.dot_general(dhl[...], xh[k], NT, preferred_element_type=F32)
        low = lax.dot_general(dhl[pl.ds(0, C)], xl[k], NT, preferred_element_type=F32)
        g = hilo[:C] + (hilo[C:] + low)
        for h in (0, 1):
            for q in (0, 1):
                sums[h, pl.ds(M * k + 16 * q, 16)] = g[L * h : L * h + L, L * q : L * q + L].reshape(16, 8, L)
        block = pl.ds(M * k, M)
        core.append(send(sums.at[1 - c, block], rc.at[block], cs.at[i], cr.at[i], sibling))

    def combine(i, k):
        core[i].wait_recv()
        block = pl.ds(M * k, M)
        sums[c, block] = sums[c, block] + rc[block]
        if i == 0:
            for d in zorder:
                part = sums.at[c, pl.ds(B0 + GB * lax.rem(z + d, Z), GB)]
                p1b.append(send(part, rb1.at[d - 1], bs1.at[d - 1], br1.at[d - 1], zpeer(d)))
        elif i <= 3:
            d = xorder[i - 1]
            p1a.append(send(sums.at[c, block], ra1.at[d - 1], as1.at[d - 1], ar1.at[d - 1], xpeer(d)))

    for i in (0, 1, 2):
        multiply(i, order[i])
    combine(0, order[0])
    multiply(3, order[3])
    combine(1, order[1])
    multiply(4, order[4])
    for i in (2, 3, 4):
        combine(i, order[i])

    def dsplit():
        return dhl[pl.ds(0, C)], dhl[pl.ds(C, C)]

    igv[...] = cotv[...] + mm3(get(ath, atl, 4), dsplit(), NN)
    for copy in p1a:
        copy.wait_recv()
    s2a[...] = sums[c, pl.ds(GA * x, GA)] + sum(ra1[d - 1] for d in xs_)
    p2a = [
        send(s2a.at[pl.ds(NA * lax.rem(z + d, Z), NA)], ra2.at[d - 1], as2.at[d - 1], ar2.at[d - 1], zpeer(d))
        for d in zorder
    ]
    for copy in p1b:
        copy.wait_recv()
    s2b[...] = sums[c, pl.ds(B0 + GB * z, GB)] + sum(rb1[d - 1] for d in zs_)
    p2b = [
        send(s2b.at[pl.ds(NB * lax.rem(x + d, X), NB)], rb2.at[d - 1], bs2.at[d - 1], br2.at[d - 1], xpeer(d))
        for d in xorder
    ]

    df[0].wait_recv()
    df[1].wait_recv()
    acc = mm3(get(ath, atl, 0), split(dfar[1] * has_up), NN) + mm3(get(ath, atl, 1), split(dfar[0] * has_down), NN)
    igv[...] = igv[...] + acc

    for copy in p2a + p2b:
        copy.wait_recv()
    mine = ry.at[y]
    mine[pl.ds(0, NA)] = s2a[pl.ds(NA * z, NA)] + sum(ra2[d - 1] for d in zs_)
    mine[pl.ds(NA, NB)] = s2b[pl.ds(NB * x, NB)] + sum(rb2[d - 1] for d in xs_)
    p3 = [send(mine, ry.at[y], ys.at[d - 1], yr.at[d - 1], ypeer(d)) for d in yorder]
    dn = [
        send(dz.at[:, pl.ds(L, L)], dnear.at[0], ds.at[2], dr.at[2], later),
        send(dz.at[:, pl.ds(0, L)], dnear.at[1], ds.at[3], dr.at[3], earlier),
    ]
    for copy in p3:
        copy.wait_recv()
    summed = ry[0]
    for k in range(1, Y):
        summed = summed + ry[k]
    fa = full.at[c, pl.ds(GA * x + NA * z, NA)]
    fb = full.at[c, pl.ds(B0 + GB * z + NB * x, NB)]
    fa[...] = summed[:NA]
    fb[...] = summed[NA:]

    g1a = {d: send(fa, fa, gas1.at[d - 1], gar1.at[d - 1], zpeer(d)) for d in zorder}
    g1b = [send(fb, fb, gbs1.at[d - 1], gbr1.at[d - 1], xpeer(d)) for d in xorder]

    def piece_a(d, j):
        return full.at[c, pl.ds(GA * lax.rem(x - d + X, X) + NA * lax.rem(z - j + Z, Z), NA)]

    def block_b(d):
        return full.at[c, pl.ds(B0 + GB * lax.rem(z - d + Z, Z), GB)]

    g2a, g2b, forward_a, forward_b = {}, {}, {}, {}

    def pass_a(d, j):
        piece = piece_a(d, j)
        forward_a[d, j] = send(piece, piece, fas.at[d, j], far_.at[d, j], sibling)
        if d == 0:
            for e in (1, 3, 2):
                g2a[e, j] = send(piece, piece, gas2.at[e - 1, j], gar2.at[e - 1, j], xpeer(e))

    def pass_b(d):
        block = block_b(d)
        forward_b[d] = send(block, block, fbs.at[d], fbr.at[d], sibling)
        if d == 0:
            for e in zorder:
                g2b[e] = send(block, block, gbs2.at[e - 1], gbr2.at[e - 1], zpeer(e))

    pass_a(0, 0)
    dn[0].wait_recv()
    dn[1].wait_recv()
    back, ahead = shifted(dz[:, :L], dz[:, L:], dnear[0] * has_earlier, dnear[1] * has_later)
    acc = mm3(get(ath, atl, 2), split(ahead), NN) + mm3(get(ath, atl, 3), split(back), NN)
    igv[...] = igv[...] + acc

    near_first = [1, 7, 2, 6, 3, 5, 4]
    for j in near_first[:2]:
        g1a[j].wait_recv()
        pass_a(0, j)
    for copy in g1b:
        copy.wait_recv()
    pass_b(0)
    for j in near_first[2:]:
        g1a[j].wait_recv()
        pass_a(0, j)

    def products(m):
        branch, tap = m // 2, 2 * lax.rem(m, 2)
        g = gathered(full, scale, m)
        grads[branch, tap] = mm3(get(jth, jtl, branch), g, NN)
        joins[branch] = joins[branch] + mm3(g, get(th, tl, 3 * branch + tap), NT)

    joins[...] = jnp.zeros_like(joins)
    for j in [0] + near_first:
        for d in (1, 3):
            g2a[d, j].wait_recv()
            pass_a(d, j)
        if j:
            g2b[j].wait_recv()
            pass_b(j)
    for j in [0] + near_first:
        g2a[2, j].wait_recv()
        pass_a(2, j)
    for d in (0, 1, 3, 2):
        for j in range(Z):
            forward_a[d, j].wait_recv()
        products(lax.rem(x - d + X, X))
    for copy in forward_b.values():
        copy.wait_recv()
    for copy in started:
        copy.wait_send()


def finish(scale, igv, grads, joins, full, th, tl, jth, jtl, ig_out, far_out, near_out, join_out, centre, joined, osem):
    copies = []

    def store(src, dst):
        copy = pltpu.make_async_copy(src, dst, osem.at[len(copies)])
        copy.start()
        copies.append(copy)

    store(igv, ig_out)
    outs = (far_out, near_out)
    for branch in (0, 1):
        for tap in (0, 2):
            store(grads.at[branch, tap], outs[branch].at[tap])
    g = gathered(full, scale, 4)
    for branch in (0, 1):
        joined[branch] = joins[branch] + mm3(g, (th[3 * branch + 1], tl[3 * branch + 1]), NT)
        store(joined.at[branch], join_out.at[:, pl.ds(C * branch, C)])
    for branch in (0, 1):
        centre[branch] = mm3((jth[branch], jtl[branch]), g, NN)
        store(centre.at[branch], outs[branch].at[1])
    for copy in copies:
        copy.wait()


def on_device(inputs, cotangent, taps_far, taps_near, joining):
    scale = 1.0 / math.sqrt(inputs.shape[1] * lax.axis_size("tm"))
    sq = (C, C)
    vm = lambda *shape: pltpu.VMEM(shape, F32)
    vb = lambda *shape: pltpu.VMEM(shape, BF16)
    dma = lambda *n: pltpu.SemaphoreType.DMA(n)
    anywhere = pl.BlockSpec(memory_space=pl.ANY)
    held = pl.BlockSpec(memory_space=pltpu.VMEM)
    scratch = (
        [vm(*sq), vm(*sq), vm(3, *sq), vm(3, *sq), vm(C, 2 * C)]
        + [vm(2, *sq), vm(2, C, L), vm(2, *sq), vm(2, C, L), vm(*sq)]
        + [vb(5, *sq)] * 4 + [vb(5, *sq)] * 2 + [vb(2 * C, C)]
        + [vm(*sq)]
        + [vm(2, 160, 8, L), vm(160, 8, L)]
        + [vm(X - 1, GA, 8, L), vm(Z - 1, GB, 8, L), vm(GA, 8, L), vm(GB, 8, L)]
        + [vm(Z - 1, NA, 8, L), vm(X - 1, NB, 8, L), vm(Y, NA + NB, 8, L)]
        + [dma(5), dma(4), dma(4), dma(4), dma(4), dma(5), dma(5)]
        + [dma(X - 1)] * 2 + [dma(Z - 1)] * 2 + [dma(Z - 1)] * 2 + [dma(X - 1)] * 2 + [dma(Y - 1)] * 2
        + [dma(Z - 1)] * 2 + [dma(X - 1)] * 2 + [dma(X - 1, Z)] * 2 + [dma(Z - 1)] * 2
        + [dma(X, Z)] * 2 + [dma(Z)] * 2
    )
    args = [pltpu.with_memory_space_constraint(v, pltpu.HBM) for v in (inputs, cotangent, taps_far, taps_near, joining)]
    shape = jax.ShapeDtypeStruct
    passed = pl.pallas_call(
        functools.partial(kernel, scale),
        out_shape=[
            shape(sq, F32), shape((2, 3, *sq), F32), shape((2, *sq), F32), shape((2, 160, 8, L), F32), shape((6, *sq), BF16), shape((6, *sq), BF16),
            shape((2, *sq), BF16), shape((2, *sq), BF16),
        ],
        in_specs=[anywhere] * 5,
        out_specs=[held] * 8,
        scratch_shapes=scratch,
        compiler_params=pltpu.CompilerParams(
            collective_id=0, has_side_effects=True, vmem_limit_bytes=32 * 1024 * 1024
        ),
    )(*args)
    return pl.pallas_call(
        functools.partial(finish, scale),
        out_shape=[shape(sq, F32), shape((3, *sq), F32), shape((3, *sq), F32), shape((C, 2 * C), F32)],
        in_specs=[held] * 8,
        out_specs=[anywhere] * 4,
        scratch_shapes=[vm(2, *sq), vm(2, *sq), dma(9)],
        compiler_params=pltpu.CompilerParams(vmem_limit_bytes=32 * 1024 * 1024),
    )(*passed)


def solution(mesh):
    in_specs = (P(None, "tm"), P(None, "tm"), P(), P(), P())
    out_specs = (P(None, "tm"), P(), P(), P())
    return jax.shard_map(
        on_device, mesh=mesh, in_specs=in_specs, out_specs=out_specs, check_vma=False
    )
```

```python
import functools
import math

import jax
import jax.numpy as jnp
from jax import lax
from jax.experimental import pallas as pl
from jax.experimental.pallas import tpu as pltpu
from jax.sharding import PartitionSpec as P

NEAR = 4
C = 256
L = 128
Y, X, Z = 8, 4, 8
MESH = pl.DeviceIdType.MESH
F32 = jnp.float32
BF16 = jnp.bfloat16
M = 32
NA = 4 * M // (X * Z)
NB = M // (X * Z)
B0 = 4 * M
GA, GB = NA * Z, NB * X
NN = (((1,), (0,)), ((), ()))
NT = (((1,), (1,)), ((), ()))


def split(v):
    hi = v.astype(BF16)
    return hi, (v - hi.astype(F32)).astype(BF16)


def mm3(a, b, dims):
    dot = functools.partial(lax.dot_general, dimension_numbers=dims, preferred_element_type=F32)
    both = dot(jnp.concatenate(a, axis=0), b[0])
    return both[:C] + (both[C:] + dot(a[0], b[1]))


def gelu_slope(value):
    inner = 0.7978845608 * (value + 0.044715 * value * value * value)
    hyper = jnp.tanh(inner)
    return 0.5 * (1.0 + hyper) + 0.5 * value * (1.0 - hyper * hyper) * 0.7978845608 * (
        1.0 + 3.0 * 0.044715 * value * value
    )


def shifted(b0, b1, p, n):
    lane = lax.broadcasted_iota(jnp.int32, (C, L), 1)
    low, high = lane < NEAR, lane >= L - NEAR
    r0, r1, rp = (pltpu.roll(v, NEAR, 1) for v in (b0, b1, p))
    s0, s1, sn = (pltpu.roll(v, L - NEAR, 1) for v in (b0, b1, n))
    back = jnp.concatenate([jnp.where(low, rp, r0), jnp.where(low, r0, r1)], axis=1)
    ahead = jnp.concatenate([jnp.where(high, s1, s0), jnp.where(high, sn, s1)], axis=1)
    return back, ahead


def gathered(full, scale, k):
    rows = [
        jnp.concatenate([full[h, pl.ds(M * k + 16 * q, 16)].reshape(L, L) for q in (0, 1)], axis=1)
        for h in (0, 1)
    ]
    return split(jnp.concatenate(rows, axis=0) * scale)


def kernel(
    scale,
    x_in, cot_in, tf_in, tn_in, j_in,
    igv, grads, joins, full, th, tl, jth, jtl,
    xv, cotv, tfv, tnv, jv,
    xfar, xnear, dfar, dnear, dz,
    xh, xl, ah, al, ath, atl, dhl, zacc,
    sums, rc, ra1, rb1, s2a, s2b, ra2, rb2, ry,
    lsem, xs, xr, ds, dr, cs, cr,
    as1, ar1, bs1, br1, as2, ar2, bs2, br2, ys, yr,
    gas1, gar1, gbs1, gbr1, gas2, gar2, gbs2, gbr2, fas, far_, fbs, fbr,
):
    me = lax.axis_index("tm")
    c = lax.rem(me, 2)
    z = lax.rem(me // 2, Z)
    x = lax.rem(me // (2 * Z), X)
    y = me // (2 * Z * X)
    total = 2 * X * Y * Z

    def at(yy, xx, zz, cc):
        return ((yy * X + xx) * Z + zz) * 2 + cc

    def ypeer(d):
        return at(lax.rem(y + d, Y), x, z, c)

    def xpeer(d):
        return at(y, lax.rem(x + d, X), z, c)

    def zpeer(d):
        return at(y, x, lax.rem(z + d, Z), c)

    sibling = at(y, x, z, 1 - c)
    later, earlier = lax.rem(me + 1, total), lax.rem(me + total - 1, total)
    ys_, xs_, zs_ = range(1, Y), range(1, X), range(1, Z)
    zorder = [4, 3, 5, 2, 6, 1, 7]
    yorder = [4, 3, 5, 2, 6, 1, 7]
    xorder = [2, 1, 3]
    started = []

    def send(src, dst, ssem, rsem, device):
        copy = pltpu.make_async_remote_copy(
            src_ref=src, dst_ref=dst, send_sem=ssem, recv_sem=rsem, device_id=(device,), device_id_type=MESH
        )
        copy.start()
        started.append(copy)
        return copy

    def local(src, dst, sem):
        copy = pltpu.make_async_copy(src, dst, sem)
        copy.start()
        return copy

    partners = [ypeer(d) for d in ys_] + [xpeer(d) for d in xs_] + [zpeer(d) for d in zs_] + [later, earlier]
    barrier = pltpu.get_barrier_semaphore()
    for partner in partners + [at(y, x, z, 1 - c)]:
        pl.semaphore_signal(barrier, inc=1, device_id=(partner,), device_id_type=MESH)
    loads = [
        local(src, dst, lsem.at[k])
        for k, (src, dst) in enumerate(
            [(j_in, jv), (tf_in, tfv), (tn_in, tnv), (x_in, xv), (cot_in, cotv)]
        )
    ]
    pl.semaphore_wait(barrier, len(partners) + 1)

    up, down = ypeer(1), ypeer(Y - 1)
    xf = [
        send(x_in, xfar.at[0], xs.at[0], xr.at[0], up),
        send(x_in, xfar.at[1], xs.at[1], xr.at[1], down),
    ]
    xn = [
        send(x_in.at[:, pl.ds(L, L)], xnear.at[0], xs.at[2], xr.at[2], later),
        send(x_in.at[:, pl.ds(0, L)], xnear.at[1], xs.at[3], xr.at[3], earlier),
    ]
    one = lambda ok: jnp.where(ok, 1.0, 0.0).astype(F32)
    has_up, has_down = one(y < Y - 1), one(y > 0)
    has_later, has_earlier = one(me < total - 1), one(me > 0)

    def put(hi, lo, k, v):
        hi[k], lo[k] = split(v)

    def get(hi, lo, k):
        return hi[k], lo[k]

    for copy in loads[:3]:
        copy.wait()
    jf, jn = split(jv[:, :C]), split(jv[:, C:])
    for k in range(3):
        put(th, tl, k, tfv[k])
        put(th, tl, 3 + k, tnv[k])
    joined = [
        mm3(jf, get(th, tl, 0), NN),
        mm3(jf, get(th, tl, 2), NN),
        mm3(jn, get(th, tl, 3), NN),
        mm3(jn, get(th, tl, 5), NN),
        mm3(jf, get(th, tl, 1), NN) + mm3(jn, get(th, tl, 4), NN),
    ]
    for k, v in enumerate(joined):
        put(ah, al, k, v)
    for copy in loads[3:]:
        copy.wait()
    put(xh, xl, 4, xv[...])
    xn[0].wait_recv()
    xn[1].wait_recv()
    back, ahead = shifted(xv[:, :L], xv[:, L:], xnear[0] * has_earlier, xnear[1] * has_later)
    put(xh, xl, 2, back)
    put(xh, xl, 3, ahead)
    zacc[...] = sum(mm3(get(ah, al, k), get(xh, xl, k), NN) for k in (4, 2, 3))
    for k, v in enumerate(joined):
        put(ath, atl, k, v.T)
    put(jth, jtl, 0, jv[:, :C].T)
    put(jth, jtl, 1, jv[:, C:].T)

    xf[0].wait_recv()
    put(xh, xl, 0, xfar[0] * has_down)
    xf[1].wait_recv()
    put(xh, xl, 1, xfar[1] * has_up)
    zvalue = zacc[...] + (mm3(get(ah, al, 0), get(xh, xl, 0), NN) + mm3(get(ah, al, 1), get(xh, xl, 1), NN))
    dzvalue = cotv[...] * gelu_slope(zvalue)
    dz[...] = dzvalue
    dhl[pl.ds(0, C)], dhl[pl.ds(C, C)] = split(dzvalue)
    df = [
        send(dz, dfar.at[0], ds.at[0], dr.at[0], up),
        send(dz, dfar.at[1], ds.at[1], dr.at[1], down),
    ]

    order = [4] + [lax.rem(x + d, X) for d in xorder] + [x]
    core, p1a, p1b, p2a = [], {}, [], []
    far_first = zorder + [0]

    def multiply(i, k):
        hilo = lax.dot_general(dhl[...], xh[k], NT, preferred_element_type=F32)
        low = lax.dot_general(dhl[pl.ds(0, C)], xl[k], NT, preferred_element_type=F32)
        g = hilo[:C] + (hilo[C:] + low)
        for h in (0, 1):
            for q in (0, 1):
                sums[h, pl.ds(M * k + 16 * q, 16)] = g[L * h : L * h + L, L * q : L * q + L].reshape(16, 8, L)
        block = pl.ds(M * k, M)
        core.append(send(sums.at[1 - c, block], rc.at[block], cs.at[i], cr.at[i], sibling))

    def combine(i, k):
        core[i].wait_recv()
        block = pl.ds(M * k, M)
        sums[c, block] = sums[c, block] + rc[block]
        if i == 0:
            for d in zorder:
                part = sums.at[c, pl.ds(B0 + GB * lax.rem(z + d, Z), GB)]
                p1b.append(send(part, rb1.at[d - 1], bs1.at[d - 1], br1.at[d - 1], zpeer(d)))
        elif i <= 3:
            d = xorder[i - 1]
            for j in far_first:
                zz = NA * lax.rem(z + j, Z)
                part = sums.at[c, pl.ds(M * k + zz, NA)]
                p1a[d, j] = send(part, ra1.at[d - 1, pl.ds(zz, NA)], as1.at[d - 1, j], ar1.at[d - 1, j], xpeer(d))

    for i in (0, 1, 2):
        multiply(i, order[i])
    combine(0, order[0])
    multiply(3, order[3])
    combine(1, order[1])
    multiply(4, order[4])
    for i in (2, 3, 4):
        combine(i, order[i])

    def dsplit():
        return dhl[pl.ds(0, C)], dhl[pl.ds(C, C)]

    for j in far_first:
        for d in xorder:
            p1a[d, j].wait_recv()
        zz = NA * lax.rem(z + j, Z)
        piece = pl.ds(zz, NA)
        s2a[piece] = sums[c, pl.ds(GA * x + zz, NA)] + sum(ra1[d - 1, piece] for d in xs_)
        if j:
            p2a.append(send(s2a.at[piece], ra2.at[j - 1], as2.at[j - 1], ar2.at[j - 1], zpeer(j)))
    for copy in p1b:
        copy.wait_recv()
    s2b[...] = sums[c, pl.ds(B0 + GB * z, GB)] + sum(rb1[d - 1] for d in zs_)
    p2b = [
        send(s2b.at[pl.ds(NB * lax.rem(x + d, X), NB)], rb2.at[d - 1], bs2.at[d - 1], br2.at[d - 1], xpeer(d))
        for d in xorder
    ]

    igv[...] = cotv[...] + mm3(get(ath, atl, 4), dsplit(), NN)
    df[0].wait_recv()
    df[1].wait_recv()
    acc = mm3(get(ath, atl, 0), split(dfar[1] * has_up), NN) + mm3(get(ath, atl, 1), split(dfar[0] * has_down), NN)
    igv[...] = igv[...] + acc

    for copy in p2a + p2b:
        copy.wait_recv()
    mine = ry.at[y]
    mine[pl.ds(0, NA)] = s2a[pl.ds(NA * z, NA)] + sum(ra2[d - 1] for d in zs_)
    mine[pl.ds(NA, NB)] = s2b[pl.ds(NB * x, NB)] + sum(rb2[d - 1] for d in xs_)
    p3 = [send(mine, ry.at[y], ys.at[d - 1], yr.at[d - 1], ypeer(d)) for d in yorder]
    dn = [
        send(dz.at[:, pl.ds(L, L)], dnear.at[0], ds.at[2], dr.at[2], later),
        send(dz.at[:, pl.ds(0, L)], dnear.at[1], ds.at[3], dr.at[3], earlier),
    ]
    for copy in p3:
        copy.wait_recv()
    summed = ry[0]
    for k in range(1, Y):
        summed = summed + ry[k]
    fa = full.at[c, pl.ds(GA * x + NA * z, NA)]
    fb = full.at[c, pl.ds(B0 + GB * z + NB * x, NB)]
    fa[...] = summed[:NA]
    fb[...] = summed[NA:]

    g1a = {d: send(fa, fa, gas1.at[d - 1], gar1.at[d - 1], zpeer(d)) for d in zorder}
    g1b = [send(fb, fb, gbs1.at[d - 1], gbr1.at[d - 1], xpeer(d)) for d in xorder]

    def piece_a(d, j):
        return full.at[c, pl.ds(GA * lax.rem(x - d + X, X) + NA * lax.rem(z - j + Z, Z), NA)]

    def block_b(d):
        return full.at[c, pl.ds(B0 + GB * lax.rem(z - d + Z, Z), GB)]

    g2a, g2b, forward_a, forward_b = {}, {}, {}, {}

    def pass_a(d, j):
        piece = piece_a(d, j)
        forward_a[d, j] = send(piece, piece, fas.at[d, j], far_.at[d, j], sibling)
        if d == 0:
            for e in (1, 3, 2):
                g2a[e, j] = send(piece, piece, gas2.at[e - 1, j], gar2.at[e - 1, j], xpeer(e))

    def pass_b(d):
        block = block_b(d)
        forward_b[d] = send(block, block, fbs.at[d], fbr.at[d], sibling)
        if d == 0:
            for e in zorder:
                g2b[e] = send(block, block, gbs2.at[e - 1], gbr2.at[e - 1], zpeer(e))

    pass_a(0, 0)
    dn[0].wait_recv()
    dn[1].wait_recv()
    back, ahead = shifted(dz[:, :L], dz[:, L:], dnear[0] * has_earlier, dnear[1] * has_later)
    acc = mm3(get(ath, atl, 2), split(ahead), NN) + mm3(get(ath, atl, 3), split(back), NN)
    igv[...] = igv[...] + acc

    near_first = [1, 7, 2, 6, 3, 5, 4]
    for j in near_first[:2]:
        g1a[j].wait_recv()
        pass_a(0, j)
    for copy in g1b:
        copy.wait_recv()
    pass_b(0)
    for j in near_first[2:]:
        g1a[j].wait_recv()
        pass_a(0, j)

    def products(m):
        branch, tap = m // 2, 2 * lax.rem(m, 2)
        g = gathered(full, scale, m)
        grads[branch, tap] = mm3(get(jth, jtl, branch), g, NN)
        joins[branch] = joins[branch] + mm3(g, get(th, tl, 3 * branch + tap), NT)

    joins[...] = jnp.zeros_like(joins)
    for j in [0] + near_first:
        for d in (1, 3):
            g2a[d, j].wait_recv()
            pass_a(d, j)
        if j:
            g2b[j].wait_recv()
            pass_b(j)
    for j in [0] + near_first:
        g2a[2, j].wait_recv()
        pass_a(2, j)
    for d in (0, 1, 3, 2):
        for j in range(Z):
            forward_a[d, j].wait_recv()
        products(lax.rem(x - d + X, X))
    for copy in forward_b.values():
        copy.wait_recv()
    for copy in started:
        copy.wait_send()


def finish(scale, igv, grads, joins, full, th, tl, jth, jtl, ig_out, far_out, near_out, join_out, centre, joined, osem):
    copies = []

    def store(src, dst):
        copy = pltpu.make_async_copy(src, dst, osem.at[len(copies)])
        copy.start()
        copies.append(copy)

    store(igv, ig_out)
    outs = (far_out, near_out)
    for branch in (0, 1):
        for tap in (0, 2):
            store(grads.at[branch, tap], outs[branch].at[tap])
    g = gathered(full, scale, 4)
    for branch in (0, 1):
        joined[branch] = joins[branch] + mm3(g, (th[3 * branch + 1], tl[3 * branch + 1]), NT)
        store(joined.at[branch], join_out.at[:, pl.ds(C * branch, C)])
    for branch in (0, 1):
        centre[branch] = mm3((jth[branch], jtl[branch]), g, NN)
        store(centre.at[branch], outs[branch].at[1])
    for copy in copies:
        copy.wait()


def on_device(inputs, cotangent, taps_far, taps_near, joining):
    scale = 1.0 / math.sqrt(inputs.shape[1] * lax.axis_size("tm"))
    sq = (C, C)
    vm = lambda *shape: pltpu.VMEM(shape, F32)
    vb = lambda *shape: pltpu.VMEM(shape, BF16)
    dma = lambda *n: pltpu.SemaphoreType.DMA(n)
    anywhere = pl.BlockSpec(memory_space=pl.ANY)
    held = pl.BlockSpec(memory_space=pltpu.VMEM)
    scratch = (
        [vm(*sq), vm(*sq), vm(3, *sq), vm(3, *sq), vm(C, 2 * C)]
        + [vm(2, *sq), vm(2, C, L), vm(2, *sq), vm(2, C, L), vm(*sq)]
        + [vb(5, *sq)] * 4 + [vb(5, *sq)] * 2 + [vb(2 * C, C)]
        + [vm(*sq)]
        + [vm(2, 160, 8, L), vm(160, 8, L)]
        + [vm(X - 1, GA, 8, L), vm(Z - 1, GB, 8, L), vm(GA, 8, L), vm(GB, 8, L)]
        + [vm(Z - 1, NA, 8, L), vm(X - 1, NB, 8, L), vm(Y, NA + NB, 8, L)]
        + [dma(5), dma(4), dma(4), dma(4), dma(4), dma(5), dma(5)]
        + [dma(X - 1, Z)] * 2 + [dma(Z - 1)] * 2 + [dma(Z - 1)] * 2 + [dma(X - 1)] * 2 + [dma(Y - 1)] * 2
        + [dma(Z - 1)] * 2 + [dma(X - 1)] * 2 + [dma(X - 1, Z)] * 2 + [dma(Z - 1)] * 2
        + [dma(X, Z)] * 2 + [dma(Z)] * 2
    )
    args = [pltpu.with_memory_space_constraint(v, pltpu.HBM) for v in (inputs, cotangent, taps_far, taps_near, joining)]
    shape = jax.ShapeDtypeStruct
    passed = pl.pallas_call(
        functools.partial(kernel, scale),
        out_shape=[
            shape(sq, F32), shape((2, 3, *sq), F32), shape((2, *sq), F32), shape((2, 160, 8, L), F32), shape((6, *sq), BF16), shape((6, *sq), BF16),
            shape((2, *sq), BF16), shape((2, *sq), BF16),
        ],
        in_specs=[anywhere] * 5,
        out_specs=[held] * 8,
        scratch_shapes=scratch,
        compiler_params=pltpu.CompilerParams(
            collective_id=0, has_side_effects=True, vmem_limit_bytes=32 * 1024 * 1024
        ),
    )(*args)
    return pl.pallas_call(
        functools.partial(finish, scale),
        out_shape=[shape(sq, F32), shape((3, *sq), F32), shape((3, *sq), F32), shape((C, 2 * C), F32)],
        in_specs=[held] * 8,
        out_specs=[anywhere] * 4,
        scratch_shapes=[vm(2, *sq), vm(2, *sq), dma(9)],
        compiler_params=pltpu.CompilerParams(vmem_limit_bytes=32 * 1024 * 1024),
    )(*passed)


def solution(mesh):
    in_specs = (P(None, "tm"), P(None, "tm"), P(), P(), P())
    out_specs = (P(None, "tm"), P(), P(), P())
    return jax.shard_map(
        on_device, mesh=mesh, in_specs=in_specs, out_specs=out_specs, check_vma=False
    )
```
